256 devices in a mesh: rows: 64 (over z, x, core), tm: 4 (over y).
Axes of the slice: x: 4, y: 4, z: 8, core: 2. Of those that a mesh axis runs over, the one named last changes fastest.
Arguments:
- features: bfloat16 [8, 128, 160, 384], P('tm', 'rows'), may hold values from -16 to 16
- cotangent: bfloat16 [8, 128, 160, 384], P('tm', 'rows'), may hold values from -6 to 6
- gamma: float32 [384], replicated, may hold values from 0.5 to 2
- kernel: bfloat16 [384, 27, 384], replicated, may hold values from -0.0625 to 0.0625
Outputs:
- input_grad: bfloat16 [8, 128, 160, 384], P('tm', 'rows')
- weight_grad: float32 [384, 27, 384], P('tm', None, 'rows')
The draws below stay inside these ranges and needn't reach their ends.
All inputs are finite; a program needn't handle non-finite values.
Results may differ from the reference program's by a relative error of at most 0.0029.
Values may be sent and summed in bfloat16 or wider, within the bound.
No kernel may reach another device: no remote copies, remote signals or barrier semaphores. Data moves between devices by JAX's collectives and lax.ppermute only.
A program may use at most 192 MiB of HBM per device.

```python
import math
import jax
import jax.numpy as jnp
from jax import lax

C = 384
TAPS = 27
COLS = 160
FRAMES = 8
HEIGHT = 128


def raised(array, stream_key, source, target, parts, factor):
    owner, partner = [(jnp.arange(array.shape[position]) // (array.shape[position] // parts)).reshape([-1 if axis == position else 1 for axis in range(array.ndim)]) for position in (source, target)]
    chosen = jax.random.permutation(stream_key, parts)[partner]
    strong = (owner == chosen) | (owner == (partner + parts // 2) % parts)
    return jnp.where(strong, factor * array, array)


def block_scale(stream_key, extent, split, low, top_value):
    level, own = 1.0, jax.random.fold_in(stream_key, 6)
    for axis_at, shards_of in split:
        draws = jnp.exp(jax.random.uniform(jax.random.fold_in(own, axis_at), (shards_of,), jnp.float32, low / len(split), top_value / len(split)))
        level = level * jnp.repeat(draws, extent[axis_at] // shards_of).reshape([-1 if axis == axis_at else 1 for axis in range(len(extent))])
    return level


def scatter_about(key, shape, scale, limit, pieces=(), held_as=jnp.bfloat16):
    loudness = block_scale(key, shape, pieces, -0.22, 0.18) if pieces else 1.0
    array = jax.random.normal(key, shape, jnp.float32) * scale * loudness
    return jnp.minimum(jnp.maximum(array, -limit), limit).astype(held_as)


def heavy_noise(stream_key, extent, deviation, reach, split, heavy, kind=jnp.bfloat16):
    entries = deviation * jax.random.normal(stream_key, extent, jnp.float32)
    if split:
        entries = entries * block_scale(stream_key, extent, split, -0.22, 0.18)
    return jnp.clip(raised(entries, jax.random.fold_in(stream_key, 3), *heavy), -reach, reach).astype(kind)


def setup_inputs(seed: int = 0) -> dict:
    keys = jax.random.split(jax.random.key(seed), 5)
    return {
        "features": heavy_noise(keys[0], (FRAMES, HEIGHT, COLS, C), 1.0, 16.0, ((0, 4), (1, 64)), (1, 3, 64, 4.0)),
        "cotangent": scatter_about(keys[1], (FRAMES, HEIGHT, COLS, C), 1.0, 6.0, ((0, 4), (1, 64))),
        "gamma": jnp.clip(jnp.exp(jax.random.uniform(keys[2], (C,), jnp.float32, math.log(0.5), math.log(2.0))), 0.5, 2.0),
        "kernel": scatter_about(keys[3], (C, TAPS, C), (TAPS * C) ** -0.5, 0.0625),
    }


def normalize(values, gamma):
    floats = values.astype(jnp.float32)
    inverse = lax.rsqrt(lax.optimization_barrier(jnp.mean(floats * floats, axis=-1, keepdims=True)) + 1e-06)
    normed = floats * inverse
    return (normed, normed * gamma, inverse)

def reference(features, cotangent, gamma, kernel):
    width = features.shape[3]
    normed, pre_act, inverse = normalize(features, gamma)
    active = jax.nn.silu(pre_act).astype(jnp.bfloat16)
    padded = jnp.pad(active, ((2, 0), (1, 1), (1, 1), (0, 0)))
    cot_pad = jnp.pad(cotangent, ((0, 2), (1, 1), (1, 1), (0, 0)))
    cot_rows = cotangent.reshape(-1, width)
    grad_act = jnp.zeros((cot_rows.shape[0], width), jnp.float32)
    tap_grads = []
    for time_tap in range(3):
        for row_tap in range(3):
            for col_tap in range(3):
                tap_index = (time_tap * 3 + row_tap) * 3 + col_tap
                window = padded[time_tap:time_tap + FRAMES, row_tap:row_tap + HEIGHT, col_tap:col_tap + COLS].reshape(-1, width)
                tap_grads.append(lax.dot_general(window, cot_rows, (((0,), (0,)), ((), ())), preferred_element_type=jnp.float32))
                cot_window = cot_pad[2 - time_tap:2 - time_tap + FRAMES, 2 - row_tap:2 - row_tap + HEIGHT, 2 - col_tap:2 - col_tap + COLS].reshape(-1, width)
                grad_act = grad_act + lax.dot_general(cot_window, kernel[:, tap_index, :], (((1,), (1,)), ((), ())), preferred_element_type=jnp.float32)
    weight_grad = jnp.stack(tap_grads, 1) * (1.0 / math.sqrt(FRAMES * HEIGHT * COLS))
    grad_act = grad_act.reshape(features.shape)
    sigma = jax.nn.sigmoid(pre_act)
    grad_pre = grad_act * sigma * (1.0 + pre_act * (1.0 - sigma))
    grad_norm = grad_pre * gamma
    input_grad = inverse * (grad_norm - normed * lax.optimization_barrier(jnp.mean(grad_norm * normed, axis=-1, keepdims=True)))
    return (input_grad.astype(jnp.bfloat16), weight_grad)
```

```python
import functools
import math

import jax
import jax.numpy as jnp
import numpy as np
from jax import lax
from jax.experimental import pallas as pl
from jax.experimental.pallas import tpu as pltpu
from jax.sharding import PartitionSpec as P

F32, BF16 = jnp.float32, jnp.bfloat16
VMEM_LIMIT = 60 * 1024 * 1024
C, COLS, PART, LANES = 384, 160, 96, 128
ZS, XS, YS, SLOTS = 8, 4, 4, 14
NT = (((1,), (1,)), ((), ()))


def rows_perm(move):
    pairs = []
    for z in range(ZS):
        for x in range(XS):
            for c in range(2):
                z2, x2, c2 = move(z, x, c)
                pairs.append(((z * XS + x) * 2 + c, (z2 * XS + x2) * 2 + c2))
    return pairs


def z_shift(steps):
    return rows_perm(lambda z, x, c: ((z + steps) % ZS, x, c))


def x_shift(steps):
    return rows_perm(lambda z, x, c: (z, (x + steps) % XS, c))


def core_swap():
    return rows_perm(lambda z, x, c: (z, x, 1 - c))


def y_shift(steps):
    return [(i, (i + steps) % YS) for i in range(YS)]


def line(count, steps):
    return [(i, i + steps) for i in range(count) if 0 <= i + steps < count]


def activation_kernel(features_ref, gamma_ref, out_ref):
    floats = features_ref[...].astype(F32)
    inverse = lax.rsqrt(jnp.mean(floats * floats, axis=-1, keepdims=True) + 1e-6)
    pre_act = floats * inverse * gamma_ref[...]
    active = pre_act * jax.nn.sigmoid(pre_act)
    blank = jnp.zeros((active.shape[0], LANES - PART), F32)
    for part in range(YS):
        piece = active[:, part * PART : (part + 1) * PART]
        out_ref[part] = jnp.concatenate([piece, blank], axis=1).astype(BF16)


def activations(features, gamma):
    pixels = features.shape[0]
    return pl.pallas_call(
        activation_kernel,
        out_shape=jax.ShapeDtypeStruct((YS, pixels, LANES), BF16),
        compiler_params=pltpu.CompilerParams(vmem_limit_bytes=VMEM_LIMIT),
    )(features, gamma)


def weight_kernel(meta_ref, c3, c2, c1, c0, a3, a2, a1, a0, up, dn, order_ref, own, send, same, before, cot, acc):
    y, core = meta_ref[0], meta_ref[1]
    cots, acts = (c0, c1, c2, c3), (a0, a1, a2, a3)
    column = lax.broadcasted_iota(jnp.int32, (4 * COLS, LANES), 0) % COLS
    for k in range(4):
        place = 3 - k
        for f in range(2):
            value = jnp.concatenate(
                [up[k, f, 0], acts[k][f, 0], acts[k][f, 1], dn[k, f, 0]], axis=0
            ).astype(F32)
            left = jnp.where(column == 0, 0.0, pltpu.roll(value, 1, 0))
            right = jnp.where(column == COLS - 1, 0.0, pltpu.roll(value, 4 * COLS - 1, 0))
            spread = jnp.concatenate([left, value, right], axis=1).astype(BF16)
            same[place * 2 + f] = spread
            later = (k + 3) % 4
            first = lax.rem(y - later + 4, 4) == 0
            before[(3 - later) * 2 + f] = jnp.where(first, jnp.zeros_like(spread), spread)
        block = lax.dot_general(
            order_ref[...], cots[k][...], NT, preferred_element_type=F32
        )
        cot[:, place * 640 : (place + 1) * 640] = block.astype(BF16)

    def window(a, b, low, count):
        rows, lanes = slice(b * COLS, (b + 2) * COLS), slice(low, low + count)
        pieces = []
        for place in range(4):
            for f in range(2):
                if a == 2:
                    pieces.append(same[place * 2 + f, rows, lanes])
                elif a == 0:
                    pieces.append(before[place * 2 + f, rows, lanes])
                elif f == 0:
                    pieces.append(before[place * 2 + 1, rows, lanes])
                else:
                    pieces.append(same[place * 2, rows, lanes])
        return jnp.concatenate(pieces, axis=0)

    def put(tap, value):
        half, slot = divmod(tap, SLOTS)
        rows, lanes = slice(half * 24, half * 24 + 24), slice(slot * LANES, slot * LANES + LANES)
        for c in range(2):
            chunk = value[c * 192 : (c + 1) * 192].reshape(ZS, 24, LANES)

            @pl.when(core == c)
            def _():
                own[:, rows, lanes] = chunk

            @pl.when(core != c)
            def _():
                acc[:, rows, lanes] = chunk

    def product(windows):
        return jnp.dot(cot[...], windows, preferred_element_type=F32)

    for a in range(3):
        for b in range(3):
            both = product(window(a, b, 0, 256))
            put((a * 3 + b) * 3, both[:, :LANES])
            put((a * 3 + b) * 3 + 1, both[:, LANES:])
    last = [(a, b) for a in range(3) for b in range(3)]
    for at in range(0, 9, 2):
        group = last[at : at + 2]
        result = product(jnp.concatenate([window(a, b, 256, 128) for a, b in group], axis=1))
        for n, (a, b) in enumerate(group):
            put((a * 3 + b) * 3 + 2, result[:, n * LANES : (n + 1) * LANES])
    put(27, jnp.zeros((C, LANES), F32))
    send[...] = acc[...].astype(BF16)


def weight_partials(meta, cots, acts, up, dn, order):
    shape = (ZS, 48, SLOTS * LANES)
    return pl.pallas_call(
        weight_kernel,
        in_specs=[pl.BlockSpec(memory_space=pltpu.SMEM)] + [pl.BlockSpec(memory_space=pltpu.VMEM)] * 11,
        out_specs=[pl.BlockSpec(memory_space=pltpu.VMEM)] * 2,
        out_shape=[jax.ShapeDtypeStruct(shape, F32), jax.ShapeDtypeStruct(shape, BF16)],
        scratch_shapes=[
            pltpu.VMEM((8, 4 * COLS, C), BF16),
            pltpu.VMEM((8, 4 * COLS, C), BF16),
            pltpu.VMEM((C, 2560), BF16),
            pltpu.VMEM(shape, F32),
        ],
        compiler_params=pltpu.CompilerParams(vmem_limit_bytes=VMEM_LIMIT),
        cost_estimate=pl.CostEstimate(flops=14 * 2 * 384 * 2560 * 256, bytes_accessed=8_000_000, transcendentals=0),
    )(meta, *cots[::-1], *acts[::-1], up, dn, order)


def input_kernel(meta_ref, own, following, up, dn, taps_ref, features_ref, gamma_ref, out_ref, ext, side, total):
    a, e = pl.program_id(1), pl.program_id(0)

    @pl.when((a == 0) & (e == 0))
    def _():
        keep = meta_ref[0] != 3
        for f in range(2):
            ext[f, COLS : 3 * COLS] = own[f]
            ext[f + 2, COLS : 3 * COLS] = jnp.where(keep, following[f], jnp.zeros_like(following[f]))
        for f in range(4):
            good = keep if f >= 2 else True
            ext[f, :COLS] = jnp.where(good, up[f], jnp.zeros_like(up[f]))
            ext[f, 3 * COLS :] = jnp.where(good, dn[f], jnp.zeros_like(dn[f]))

    rows = []
    for f in range(2):
        pieces = [ext[f + 2 - a, (2 - b) * COLS : (4 - b) * COLS] for b in range(3)]
        rows.append(jnp.concatenate(pieces, axis=1))
    weights = jnp.concatenate([taps_ref[0, b, 0] for b in range(3)], axis=1)
    value = lax.dot_general(jnp.concatenate(rows, axis=0), weights, NT, preferred_element_type=F32)

    @pl.when(a == 0)
    def _():
        side[...] = value

    @pl.when(a != 0)
    def _():
        side[...] += value

    column = lax.broadcasted_iota(jnp.int32, (4 * COLS, C), 0) % COLS

    @pl.when((a == 2) & (e == 0))
    def _():
        total[...] = jnp.where(column == COLS - 1, 0.0, pltpu.roll(side[...], 4 * COLS - 1, 0))

    @pl.when((a == 2) & (e == 1))
    def _():
        total[...] += side[...]

    @pl.when((a == 2) & (e == 2))
    def _():
        grad_act = total[...] + jnp.where(column == 0, 0.0, pltpu.roll(side[...], 1, 0))
        gamma = gamma_ref[...]
        floats = features_ref[...].astype(F32)
        inverse = lax.rsqrt(jnp.mean(floats * floats, axis=-1, keepdims=True) + 1e-6)
        normed = floats * inverse
        pre_act = normed * gamma
        sigma = jax.nn.sigmoid(pre_act)
        grad_norm = grad_act * sigma * (1.0 + pre_act * (1.0 - sigma)) * gamma
        inner = jnp.mean(grad_norm * normed, axis=-1, keepdims=True)
        out_ref[...] = (inverse * (grad_norm - normed * inner)).astype(BF16)


def input_gradient(meta, own, following, up, dn, taps, features, gamma):
    pixels = features.shape[0]
    whole = lambda shape: pl.BlockSpec(shape, lambda e, a: (0,) * len(shape))
    return pl.pallas_call(
        input_kernel,
        grid=(3, 3),
        in_specs=[
            pl.BlockSpec(memory_space=pltpu.SMEM),
            whole((2, 2 * COLS, C)),
            whole((2, 2 * COLS, C)),
            whole((4, COLS, C)),
            whole((4, COLS, C)),
            pl.BlockSpec((1, 3, 1, C, C), lambda e, a: (a, 0, e, 0, 0)),
            whole((pixels, C)),
            whole((1, C)),
        ],
        out_specs=whole((pixels, C)),
        out_shape=jax.ShapeDtypeStruct((pixels, C), BF16),
        scratch_shapes=[
            pltpu.VMEM((4, 4 * COLS, C), BF16),
            pltpu.VMEM((pixels, C), F32),
            pltpu.VMEM((pixels, C), F32),
        ],
        compiler_params=pltpu.CompilerParams(vmem_limit_bytes=VMEM_LIMIT),
        cost_estimate=pl.CostEstimate(flops=27 * 2 * 640 * C * C, bytes_accessed=12_000_000, transcendentals=0),
    )(meta, own, following, up, dn, taps, features, gamma)


def output_order():
    order = np.zeros((C, C), np.float32)
    for c in range(2):
        for z in range(ZS):
            for x in range(XS):
                for j in range(6):
                    order[((c * ZS + z) * XS + x) * 6 + j, ((z * XS + x) * 2 + c) * 6 + j] = 1.0
    return jnp.asarray(order, BF16)


def body(features, cotangent, gamma, kernel):
    frames, height, columns, width = features.shape
    pixels = frames * height * columns
    y, r = lax.axis_index("tm"), lax.axis_index("rows")
    z, x, core = r // (2 * XS), (r // 2) % XS, r % 2
    meta = jnp.stack([y, core]).astype(jnp.int32)
    gamma = gamma.reshape(1, width)
    flat = features.reshape(pixels, width)

    cots = [cotangent] + [lax.ppermute(cotangent, "tm", y_shift(k)) for k in (1, 2, 3)]
    taps = jnp.transpose(kernel, (1, 0, 2)).reshape(3, 3, 3, width, width)
    active = activations(flat, gamma)
    acts = [lax.dynamic_index_in_dim(active, y, 0, keepdims=False)]
    for k in (1, 2, 3):
        piece = lax.dynamic_index_in_dim(active, (y + k) % YS, 0, keepdims=False)
        acts.append(lax.ppermute(piece, "tm", y_shift(k)))
    acts = [value.reshape(2, 2, columns, LANES) for value in acts]
    stacked = jnp.stack(acts)
    act_up = lax.ppermute(stacked[:, :, 1:], "rows", line(64, 1))
    act_dn = lax.ppermute(stacked[:, :, :1], "rows", line(64, -1))
    own, send = weight_partials(
        meta, [c.reshape(pixels, width) for c in cots], acts, act_up, act_dn, output_order()
    )
    other = lax.ppermute(send, "rows", core_swap())

    following = cots[3]
    ext = jnp.concatenate([cotangent, following], axis=0)
    cot_up = lax.ppermute(ext[:, 1], "rows", line(64, 1))
    cot_dn = lax.ppermute(ext[:, 0], "rows", line(64, -1))
    input_grad = input_gradient(
        meta,
        cotangent.reshape(2, 2 * columns, width),
        following.reshape(2, 2 * columns, width),
        cot_up,
        cot_dn,
        taps,
        flat,
        gamma,
    )

    def chunk(offset):
        at = (z + offset) % ZS
        return lax.dynamic_index_in_dim(own, at, 0, keepdims=False) + lax.dynamic_index_in_dim(
            other, at, 0, keepdims=False
        ).astype(F32)

    ahead = lax.ppermute(chunk(4).astype(BF16), "rows", z_shift(1))
    behind = lax.ppermute(chunk(-3).astype(BF16), "rows", z_shift(-1))
    for step in (3, 2, 1):
        ahead = lax.ppermute((ahead.astype(F32) + chunk(step)).astype(BF16), "rows", z_shift(1))
        if step > 1:
            behind = lax.ppermute(
                (behind.astype(F32) + chunk(1 - step)).astype(BF16), "rows", z_shift(-1)
            )
    total = chunk(0) + ahead.astype(F32) + behind.astype(F32)
    total = total.reshape(2, XS, 6, SLOTS * LANES)
    mine = lax.dynamic_index_in_dim(total, x, 1, keepdims=False)
    for k in (1, 2, 3):
        piece = lax.dynamic_index_in_dim(total, (x + k) % XS, 1, keepdims=False)
        mine = mine + lax.ppermute(piece, "rows", x_shift(k))
    mine = mine.reshape(2, 6, SLOTS, LANES)[..., :PART]
    mine = jnp.transpose(mine, (3, 0, 2, 1)).reshape(PART, 2 * SLOTS, 6)[:, :27]
    count = frames * height * columns * lax.axis_size("tm") * lax.axis_size("rows")
    weight_grad = mine * (1.0 / math.sqrt(count))
    return input_grad.reshape(features.shape), weight_grad


def solution(mesh):
    placed = (P("tm", "rows", None, None), P("tm", "rows", None, None), P(), P())
    return jax.shard_map(
        body,
        mesh=mesh,
        in_specs=placed,
        out_specs=(P("tm", "rows", None, None), P("tm", None, "rows")),
        check_vma=False,
    )
```

```python
import math

import jax
import jax.numpy as jnp
from jax import lax
from jax.experimental import pallas as pl
from jax.experimental.pallas import tpu as pltpu
from jax.sharding import PartitionSpec as P

F32, BF16 = jnp.float32, jnp.bfloat16
VMEM_LIMIT = 60 * 1024 * 1024
C, COLS, PART, LANES = 384, 160, 96, 128
ZS, XS, YS = 8, 4, 4
NT = (((1,), (1,)), ((), ()))


def rows_perm(move):
    pairs = []
    for z in range(ZS):
        for x in range(XS):
            for c in range(2):
                z2, x2, c2 = move(z, x, c)
                pairs.append(((z * XS + x) * 2 + c, (z2 * XS + x2) * 2 + c2))
    return pairs


def z_shift(steps):
    return rows_perm(lambda z, x, c: ((z + steps) % ZS, x, c))


def x_shift(steps):
    return rows_perm(lambda z, x, c: (z, (x + steps) % XS, c))


def core_swap():
    return rows_perm(lambda z, x, c: (z, x, 1 - c))


def y_shift(steps):
    return [(i, (i + steps) % YS) for i in range(YS)]


def line(count, steps):
    return [(i, i + steps) for i in range(count) if 0 <= i + steps < count]


def activation_kernel(y_ref, features_ref, gamma_ref, *out_refs):
    floats = features_ref[...].astype(F32)
    inverse = lax.rsqrt(jnp.mean(floats * floats, axis=-1, keepdims=True) + 1e-6)
    pre_act = floats * inverse * gamma_ref[...][None, :]
    active = pre_act * jax.nn.sigmoid(pre_act)
    blank = jnp.zeros((active.shape[0], LANES - PART), F32)
    for part in range(YS):
        piece = active[:, part * PART : (part + 1) * PART]
        piece = jnp.concatenate([piece, blank], axis=1).astype(BF16)
        place = lax.rem(part - y_ref[0] + YS, YS)
        for k in range(YS):

            @pl.when(place == k)
            def _():
                out_refs[k][...] = piece


def activations(y, features, gamma):
    pixels = features.shape[0]
    return pl.pallas_call(
        activation_kernel,
        in_specs=[pl.BlockSpec(memory_space=pltpu.SMEM)] + [pl.BlockSpec(memory_space=pltpu.VMEM)] * 2,
        out_shape=[jax.ShapeDtypeStruct((pixels, LANES), BF16)] * YS,
        compiler_params=pltpu.CompilerParams(vmem_limit_bytes=VMEM_LIMIT),
    )(y, features, gamma)


def weight_kernel(y_ref, c3, c2a, c2b, c1, c0, a0, a1, a2, a3, up, dn, order_ref, own, send, spread, cot):
    y = y_ref[0]
    acts = (a0, a1, a2, a3)
    column = lax.broadcasted_iota(jnp.int32, (4 * COLS, LANES), 0) % COLS
    for k in range(4):
        for f in range(2):
            value = jnp.concatenate(
                [up[k, f, 0], acts[k][f, 0], acts[k][f, 1], dn[k, f, 0]], axis=0
            )
            floats = value.astype(F32)
            left = jnp.where(column == 0, 0.0, pltpu.roll(floats, 1, 0)).astype(BF16)
            right = jnp.where(column == COLS - 1, 0.0, pltpu.roll(floats, 4 * COLS - 1, 0)).astype(BF16)
            places = [(4 - k) * 2 + f] + ([f] if k == 0 else [])
            for place in places:
                rows = slice(place * 320, place * 320 + 320)
                for b in range(3):
                    for e, part in enumerate((left, value, right)):
                        at = (b * 3 + e) * LANES
                        spread[rows, at : at + LANES] = part[b * COLS : (b + 2) * COLS]
    order = order_ref[...]
    for k, pieces in enumerate(((c0,), (c1,), (c2a, c2b), (c3,))):
        first = lax.rem(y - k + 4, 4) == 0
        at = (3 - k) * 640
        for piece in pieces:
            size = piece.shape[0]
            block = lax.dot_general(order, piece[...], NT, preferred_element_type=F32).astype(BF16)
            blank = jnp.zeros_like(block)
            cot[2, :, at : at + size] = block
            cot[0, :, at : at + size] = jnp.where(first, blank, block)
            at += size
        at = (3 - k) * 640
        frame = lax.broadcasted_iota(jnp.int32, (C, 640), 1)
        block = cot[2, :, at : at + 640]
        cot[1, :, at : at + 640] = jnp.where(first & (frame < 320), jnp.zeros_like(block), block)
    pieces = []
    for a in range(3):
        value = jnp.dot(
            cot[a], spread[a * 320 : a * 320 + 2560, :], preferred_element_type=F32
        )
        pieces += [value[:, s * LANES : s * LANES + PART] for s in range(9)]
    packed = jnp.concatenate(pieces, axis=1)
    own[...] = packed[: C // 2]
    send[...] = packed[C // 2 :].astype(BF16)


def weight_partials(y, cots, acts, up, dn, order):
    shape = (C // 2, 27 * PART)
    return pl.pallas_call(
        weight_kernel,
        in_specs=[pl.BlockSpec(memory_space=pltpu.SMEM)] + [pl.BlockSpec(memory_space=pltpu.VMEM)] * 12,
        out_specs=[pl.BlockSpec(memory_space=pltpu.VMEM)] * 2,
        out_shape=[jax.ShapeDtypeStruct(shape, F32), jax.ShapeDtypeStruct(shape, BF16)],
        scratch_shapes=[
            pltpu.VMEM((10 * 320, 9 * LANES), BF16),
            pltpu.VMEM((3, C, 2560), BF16),
        ],
        compiler_params=pltpu.CompilerParams(vmem_limit_bytes=VMEM_LIMIT),
        cost_estimate=pl.CostEstimate(flops=14 * 2 * 384 * 2560 * 256, bytes_accessed=8_000_000, transcendentals=0),
    )(y, *cots, *acts, up, dn, order)


def input_kernel(y_ref, own, following, up, dn, taps_ref, features_ref, gamma_ref, out_ref, ext, side):
    a = pl.program_id(0)

    @pl.when(a == 0)
    def _():
        keep = y_ref[0] != 3
        for f in range(2):
            ext[f, COLS : 3 * COLS] = own[f]
            ext[f + 2, COLS : 3 * COLS] = jnp.where(keep, following[f], jnp.zeros_like(following[f]))
        for f in range(4):
            good = keep if f >= 2 else True
            ext[f, :COLS] = jnp.where(good, up[f], jnp.zeros_like(up[f]))
            ext[f, 3 * COLS :] = jnp.where(good, dn[f], jnp.zeros_like(dn[f]))

    rows = []
    for f in range(2):
        pieces = [ext[f + 2 - a, (2 - b) * COLS : (4 - b) * COLS] for b in range(3)]
        rows.append(jnp.concatenate(pieces, axis=1))
    weights = jnp.concatenate(
        [jnp.concatenate([taps_ref[0, b, e] for b in range(3)], axis=1) for e in range(3)], axis=0
    )
    value = lax.dot_general(jnp.concatenate(rows, axis=0), weights, NT, preferred_element_type=F32)

    @pl.when(a == 0)
    def _():
        side[...] = value

    @pl.when(a == 1)
    def _():
        side[...] += value

    @pl.when(a == 2)
    def _():
        column = lax.broadcasted_iota(jnp.int32, (4 * COLS, C), 0) % COLS
        side[...] += value
        grad_act = side[:, C : 2 * C]
        grad_act += jnp.where(column == COLS - 1, 0.0, pltpu.roll(side[:, :C], 4 * COLS - 1, 0))
        grad_act += jnp.where(column == 0, 0.0, pltpu.roll(side[:, 2 * C :], 1, 0))
        gamma = gamma_ref[...][None, :]
        floats = features_ref[...].astype(F32)
        inverse = lax.rsqrt(jnp.mean(floats * floats, axis=-1, keepdims=True) + 1e-6)
        normed = floats * inverse
        pre_act = normed * gamma
        sigma = jax.nn.sigmoid(pre_act)
        grad_norm = grad_act * sigma * (1.0 + pre_act * (1.0 - sigma)) * gamma
        inner = jnp.mean(grad_norm * normed, axis=-1, keepdims=True)
        out_ref[...] = (inverse * (grad_norm - normed * inner)).astype(BF16)


def input_gradient(y, own, following, up, dn, taps, features, gamma):
    pixels = features.shape[0]
    whole = lambda shape: pl.BlockSpec(shape, lambda a: (0,) * len(shape))
    return pl.pallas_call(
        input_kernel,
        grid=(3,),
        in_specs=[
            pl.BlockSpec(memory_space=pltpu.SMEM),
            whole((2, 2 * COLS, C)),
            whole((2, 2 * COLS, C)),
            whole((4, COLS, C)),
            whole((4, COLS, C)),
            pl.BlockSpec((1, 3, 3, C, C), lambda a: (a, 0, 0, 0, 0)),
            whole((pixels, C)),
            whole((C,)),
        ],
        out_specs=whole((pixels, C)),
        out_shape=jax.ShapeDtypeStruct((pixels, C), BF16),
        scratch_shapes=[
            pltpu.VMEM((4, 4 * COLS, C), BF16),
            pltpu.VMEM((pixels, 3 * C), F32),
        ],
        compiler_params=pltpu.CompilerParams(vmem_limit_bytes=VMEM_LIMIT),
        cost_estimate=pl.CostEstimate(flops=27 * 2 * 640 * C * C, bytes_accessed=12_000_000, transcendentals=0),
    )(y, own, following, up, dn, taps, features, gamma)


def output_order(z, x, core):
    row = jnp.arange(C)
    c2, x2, z2, j = row // 192, row // 48 % XS, row // 6 % ZS, row % 6
    bits = z2 // 4 ^ z2 // 2 % 2 * 2 ^ z2 % 2 * 6
    channel = (z ^ bits) * 48 + (x + x2) % XS * 12 + (core + c2) % 2 * 6 + j
    return (channel[:, None] == jnp.arange(C)[None, :]).astype(BF16)


def body(features, cotangent, gamma, kernel):
    frames, height, columns, width = features.shape
    pixels = frames * height * columns
    y, r = lax.axis_index("tm"), lax.axis_index("rows")
    z, x, core = r // (2 * XS), (r // 2) % XS, r % 2
    block = y.reshape(1).astype(jnp.int32)
    order = output_order(z, x, core)
    flat = features.reshape(pixels, width)
    taps = jnp.transpose(kernel, (1, 0, 2)).reshape(3, 3, 3, width, width)

    following = lax.ppermute(cotangent, "tm", y_shift(3))
    previous = lax.ppermute(cotangent, "tm", y_shift(1))
    active = activations(block, flat, gamma)
    acts = [active[0]] + [lax.ppermute(active[k], "tm", y_shift(k)) for k in (1, 2, 3)]
    acts = [value.reshape(2, 2, columns, LANES) for value in acts]
    far = [
        lax.ppermute(previous[0], "tm", y_shift(1)).reshape(pixels // 2, width),
        lax.ppermute(following[1], "tm", y_shift(3)).reshape(pixels // 2, width),
    ]
    stacked = jnp.stack(acts)
    act_up = lax.ppermute(stacked[:, :, 1:], "rows", line(64, 1))
    act_dn = lax.ppermute(stacked[:, :, :1], "rows", line(64, -1))
    cots = [following.reshape(pixels, width), *far, previous.reshape(pixels, width), cotangent.reshape(pixels, width)]
    own, send = weight_partials(block, cots, acts, act_up, act_dn, order)
    other = lax.ppermute(send, "rows", core_swap())

    def part(k):
        rows = slice(48 * k, 48 * k + 48)
        return own[rows] + other[rows].astype(F32)

    kept = part(0)
    parts = [part(k).astype(BF16) for k in (2, 1, 3)]
    block, *parts = lax.optimization_barrier((block, *parts))
    received = [lax.ppermute(value, "rows", x_shift(k)) for value, k in zip(parts, (2, 1, 3))]

    ext = jnp.concatenate([cotangent, following], axis=0)
    cot_up = lax.ppermute(ext[:, 1], "rows", line(64, 1))
    cot_dn = lax.ppermute(ext[:, 0], "rows", line(64, -1))
    input_grad = input_gradient(
        block,
        cotangent.reshape(2, 2 * columns, width),
        following.reshape(2, 2 * columns, width),
        cot_up,
        cot_dn,
        taps,
        flat,
        gamma,
    )

    input_grad, *received = lax.optimization_barrier((input_grad, *received))
    total = kept
    for value in received:
        total = total + value.astype(F32)
    for bits, wire in ((1, BF16), (2, F32), (6, F32)):
        half = total.shape[0] // 2
        pairs = rows_perm(lambda z, x, c: (z ^ bits, x, c))
        total = total[:half] + lax.ppermute(total[half:].astype(wire), "rows", pairs).astype(F32)
    mine = total.reshape(6, 27, PART)
    count = pixels * lax.axis_size("tm") * lax.axis_size("rows")
    weight_grad = jnp.transpose(mine, (2, 1, 0)) * (1.0 / math.sqrt(count))
    return input_grad.reshape(features.shape), weight_grad


def solution(mesh):
    placed = (P("tm", "rows", None, None), P("tm", "rows", None, None), P(), P())
    return jax.shard_map(
        body,
        mesh=mesh,
        in_specs=placed,
        out_specs=(P("tm", "rows", None, None), P("tm", None, "rows")),
        check_vma=False,
    )
```

```python
import math

import jax
import jax.numpy as jnp
from jax import lax
from jax.experimental import pallas as pl
from jax.experimental.pallas import tpu as pltpu
from jax.sharding import PartitionSpec as P

F32, BF16 = jnp.float32, jnp.bfloat16
VMEM_LIMIT, VMEM_SMALL = 40 * 1024 * 1024, 26 * 1024 * 1024
C, COLS, PART, LANES = 384, 160, 96, 128
ZS, XS, YS = 8, 4, 4
NT = (((1,), (1,)), ((), ()))


def rows_perm(move):
    pairs = []
    for z in range(ZS):
        for x in range(XS):
            for c in range(2):
                z2, x2, c2 = move(z, x, c)
                pairs.append(((z * XS + x) * 2 + c, (z2 * XS + x2) * 2 + c2))
    return pairs


def x_shift(steps):
    return rows_perm(lambda z, x, c: (z, (x + steps) % XS, c))


def core_swap():
    return rows_perm(lambda z, x, c: (z, x, 1 - c))


def y_shift(steps):
    return [(i, (i + steps) % YS) for i in range(YS)]


def line(count, steps):
    return [(i, i + steps) for i in range(count) if 0 <= i + steps < count]


def activation_kernel(y_ref, features_ref, gamma_ref, *out_refs):
    floats = features_ref[...].astype(F32)
    inverse = lax.rsqrt(jnp.mean(floats * floats, axis=-1, keepdims=True) + 1e-6)
    pre_act = floats * inverse * gamma_ref[...][None, :]
    active = pre_act * jax.nn.sigmoid(pre_act)
    for part in range(YS):
        lanes = slice(part * PART, (part + 1) * PART)
        lines = [active[q * COLS : (q + 1) * COLS, lanes] for q in range(4)]
        piece = jnp.concatenate(lines, axis=1).astype(BF16)
        place = lax.rem(part - y_ref[0] + YS, YS)
        for k in range(YS):

            @pl.when(place == k)
            def _():
                out_refs[k][...] = piece


def activations(y, features, gamma):
    return pl.pallas_call(
        activation_kernel,
        in_specs=[pl.BlockSpec(memory_space=pltpu.SMEM)] + [pl.BlockSpec(memory_space=pltpu.VMEM)] * 2,
        out_shape=[jax.ShapeDtypeStruct((COLS, C), BF16)] * YS,
        compiler_params=pltpu.CompilerParams(vmem_limit_bytes=VMEM_LIMIT),
    )(y, features, gamma)


def halo_kernel(a0, a1, a2, a3, up, dn):
    acts = (a0, a1, a2, a3)
    for out, h in ((up, 1), (dn, 0)):
        for f in range(2):
            at = (f * 2 + h) * PART
            lines = [act[:, at : at + PART] for act in acts]
            out[f] = jnp.concatenate(lines, axis=1)


def halo_rows(acts):
    return pl.pallas_call(
        halo_kernel,
        in_specs=[pl.BlockSpec(memory_space=pltpu.VMEM)] * 4,
        out_specs=[pl.BlockSpec(memory_space=pltpu.VMEM)] * 2,
        out_shape=[jax.ShapeDtypeStruct((2, COLS, C), BF16)] * 2,
        compiler_params=pltpu.CompilerParams(vmem_limit_bytes=VMEM_SMALL),
    )(*acts)


def spread_kernel(a0, a1, a2, a3, up, dn, spread):
    acts = (a0, a1, a2, a3)
    column = lax.broadcasted_iota(jnp.int32, (4 * COLS, LANES), 0) % COLS
    blank = jnp.zeros((4 * COLS, LANES - PART), F32)
    for k in range(4):
        for f in range(2):
            lines = [
                up[f, :, k * PART : (k + 1) * PART],
                acts[k][:, f * 2 * PART : (f * 2 + 1) * PART],
                acts[k][:, (f * 2 + 1) * PART : (f * 2 + 2) * PART],
                dn[f, :, k * PART : (k + 1) * PART],
            ]
            floats = jnp.concatenate(lines, axis=0).astype(F32)
            floats = jnp.concatenate([floats, blank], axis=1)
            value = floats.astype(BF16)
            left = jnp.where(column == 0, 0.0, pltpu.roll(floats, 1, 0)).astype(BF16)
            right = jnp.where(column == COLS - 1, 0.0, pltpu.roll(floats, 4 * COLS - 1, 0)).astype(BF16)
            places = [(4 - k) * 2 + f] + ([f] if k == 0 else [])
            for place in places:
                rows = slice(place * 320, place * 320 + 320)
                for b in range(3):
                    for e, part in enumerate((left, value, right)):
                        at = (b * 3 + e) * LANES
                        spread[rows, at : at + LANES] = part[b * COLS : (b + 2) * COLS]


def spread_windows(acts, up, dn):
    return pl.pallas_call(
        spread_kernel,
        in_specs=[pl.BlockSpec(memory_space=pltpu.VMEM)] * 6,
        out_specs=pl.BlockSpec(memory_space=pltpu.VMEM),
        out_shape=jax.ShapeDtypeStruct((10 * 320, 9 * LANES), BF16),
        compiler_params=pltpu.CompilerParams(vmem_limit_bytes=VMEM_SMALL),
    )(*acts, up, dn)


def weight_kernel(y_ref, c3, c2a, c2b, c1, c0, spread, order_ref, own, send, cot):
    y = y_ref[0]
    order = order_ref[...]
    rows = order.shape[0]
    for k, pieces in enumerate(((c0,), (c1,), (c2a, c2b), (c3,))):
        first = lax.rem(y - k + 4, 4) == 0
        blocks = [
            lax.dot_general(order, piece[...], NT, preferred_element_type=F32).astype(BF16)
            for piece in pieces
        ]
        block = blocks[0] if len(blocks) == 1 else jnp.concatenate(blocks, axis=1)
        blank = jnp.zeros_like(block)
        frame = lax.broadcasted_iota(jnp.int32, block.shape, 1)
        at = (3 - k) * 640
        cot[2, :, at : at + 640] = block
        cot[1, :, at : at + 640] = jnp.where(first & (frame < 320), blank, block)
        cot[0, :, at : at + 640] = jnp.where(first, blank, block)
    pieces = []
    for a in range(3):
        value = jnp.dot(
            cot[a], spread[a * 320 : a * 320 + 2560, :], preferred_element_type=F32
        )
        pieces += [value[:, s * LANES : s * LANES + PART] for s in range(9)]
    packed = jnp.concatenate(pieces, axis=1)
    own[...] = packed[: rows // 2]
    send[...] = packed[rows // 2 :]


def weight_partials(y, cots, spread, order):
    rows = order.shape[0]
    shape = (rows // 2, 27 * PART)
    return pl.pallas_call(
        weight_kernel,
        in_specs=[pl.BlockSpec(memory_space=pltpu.SMEM)] + [pl.BlockSpec(memory_space=pltpu.VMEM)] * 7,
        out_specs=[pl.BlockSpec(memory_space=pltpu.VMEM)] * 2,
        out_shape=[jax.ShapeDtypeStruct(shape, F32)] * 2,
        scratch_shapes=[pltpu.VMEM((3, rows, 2560), BF16)],
        compiler_params=pltpu.CompilerParams(vmem_limit_bytes=VMEM_SMALL),
        cost_estimate=pl.CostEstimate(flops=28 * rows * 2560 * 256 * 2, bytes_accessed=8_000_000, transcendentals=0),
    )(y, *cots, spread, order)


def input_kernel(y_ref, own, following, up, dn, taps_ref, features_ref, gamma_ref, out_ref, ext, side):
    a = pl.program_id(0)

    @pl.when(a == 0)
    def _():
        keep = y_ref[0] != 3
        for f in range(2):
            ext[f, COLS : 3 * COLS] = own[f]
            ext[f, :COLS] = up[f]
            ext[f, 3 * COLS :] = dn[f]
            ext[f + 2, COLS : 3 * COLS] = jnp.where(keep, following[f], jnp.zeros_like(following[f]))
            ext[f + 2, :COLS] = jnp.where(keep, up[f + 2], jnp.zeros_like(up[f + 2]))
            ext[f + 2, 3 * COLS :] = jnp.where(keep, dn[f + 2], jnp.zeros_like(dn[f + 2]))

    rows = []
    for f in range(2):
        pieces = [ext[f + 2 - a, (2 - b) * COLS : (4 - b) * COLS] for b in range(3)]
        rows.append(jnp.concatenate(pieces, axis=1))
    weights = jnp.concatenate(
        [jnp.concatenate([taps_ref[0, b, e] for b in range(3)], axis=1) for e in range(3)], axis=0
    )
    value = lax.dot_general(jnp.concatenate(rows, axis=0), weights, NT, preferred_element_type=F32)

    @pl.when(a == 0)
    def _():
        side[...] = value

    @pl.when(a == 1)
    def _():
        side[...] += value

    @pl.when(a == 2)
    def _():
        column = lax.broadcasted_iota(jnp.int32, (4 * COLS, C), 0) % COLS
        side[...] += value
        grad_act = side[:, C : 2 * C]
        grad_act += jnp.where(column == COLS - 1, 0.0, pltpu.roll(side[:, :C], 4 * COLS - 1, 0))
        grad_act += jnp.where(column == 0, 0.0, pltpu.roll(side[:, 2 * C :], 1, 0))
        gamma = gamma_ref[...][None, :]
        floats = features_ref[...].astype(F32)
        inverse = lax.rsqrt(jnp.mean(floats * floats, axis=-1, keepdims=True) + 1e-6)
        normed = floats * inverse
        pre_act = normed * gamma
        sigma = jax.nn.sigmoid(pre_act)
        grad_norm = grad_act * sigma * (1.0 + pre_act * (1.0 - sigma)) * gamma
        inner = jnp.mean(grad_norm * normed, axis=-1, keepdims=True)
        out_ref[...] = (inverse * (grad_norm - normed * inner)).astype(BF16)


def input_gradient(y, own, following, up, dn, taps, features, gamma):
    pixels = features.shape[0]
    whole = lambda shape: pl.BlockSpec(shape, lambda a: (0,) * len(shape))
    return pl.pallas_call(
        input_kernel,
        grid=(3,),
        in_specs=[
            pl.BlockSpec(memory_space=pltpu.SMEM),
            whole((2, 2 * COLS, C)),
            whole((2, 2 * COLS, C)),
            whole((4, COLS, C)),
            whole((4, COLS, C)),
            pl.BlockSpec((1, 3, 3, C, C), lambda a: (a, 0, 0, 0, 0)),
            whole((pixels, C)),
            whole((C,)),
        ],
        out_specs=whole((pixels, C)),
        out_shape=jax.ShapeDtypeStruct((pixels, C), BF16),
        scratch_shapes=[
            pltpu.VMEM((4, 4 * COLS, C), BF16),
            pltpu.VMEM((pixels, 3 * C), F32),
        ],
        compiler_params=pltpu.CompilerParams(vmem_limit_bytes=VMEM_LIMIT),
        cost_estimate=pl.CostEstimate(flops=27 * 2 * 640 * C * C, bytes_accessed=12_000_000, transcendentals=0),
    )(y, own, following, up, dn, taps, features, gamma)


def output_order(z, x, core, parts):
    row = jnp.arange(len(parts) * 96)
    c2, at, z2, j = row // (48 * len(parts)), row // 48 % len(parts), row // 6 % ZS, row % 6
    x2 = jnp.where(at == 0, parts[0], parts[1])
    bits = z2 // 4 ^ z2 // 2 % 2 * 2 ^ z2 % 2 * 6
    channel = (z ^ bits) * 48 + (x + x2) % XS * 12 + (core + c2) % 2 * 6 + j
    return (channel[:, None] == jnp.arange(C)[None, :]).astype(BF16)


def body(features, cotangent, gamma, kernel):
    frames, height, columns, width = features.shape
    pixels = frames * height * columns
    y, r = lax.axis_index("tm"), lax.axis_index("rows")
    z, x, core = r // (2 * XS), (r // 2) % XS, r % 2
    block = y.reshape(1).astype(jnp.int32)
    groups = ((2, 1), (3, 0))
    orders = [output_order(z, x, core, parts) for parts in groups]
    flat = features.reshape(pixels, width)
    taps = jnp.transpose(kernel, (1, 0, 2)).reshape(3, 3, 3, width, width)

    active = activations(block, flat, gamma)
    acts = [active[0]] + [lax.ppermute(active[k], "tm", y_shift(k)) for k in (1, 2, 3)]
    local, *acts = lax.optimization_barrier((cotangent, *acts))
    following = lax.ppermute(local, "tm", y_shift(3))
    previous = lax.ppermute(local, "tm", y_shift(1))
    rows_up, rows_dn = halo_rows(acts)
    rows_up = lax.ppermute(rows_up, "rows", line(64, 1))
    rows_dn = lax.ppermute(rows_dn, "rows", line(64, -1))
    far = [
        lax.ppermute(previous[0], "tm", y_shift(1)).reshape(pixels // 2, width),
        lax.ppermute(following[1], "tm", y_shift(3)).reshape(pixels // 2, width),
    ]
    ext = jnp.concatenate([cotangent, following], axis=0)
    cot_up = lax.ppermute(ext[:, 1], "rows", line(64, 1))
    cot_dn = lax.ppermute(ext[:, 0], "rows", line(64, -1))
    far, rows_up, rows_dn = lax.optimization_barrier((far, rows_up, rows_dn))
    spread = spread_windows(acts, rows_up, rows_dn)
    orders[1], cot_up, cot_dn = lax.optimization_barrier((orders[1], cot_up, cot_dn))
    cots = [following.reshape(pixels, width), *far, previous.reshape(pixels, width), cotangent.reshape(pixels, width)]

    own, send = weight_partials(block, cots, spread, orders[0])
    other = lax.ppermute(send, "rows", core_swap())
    orders[1], own = lax.optimization_barrier((orders[1], own))
    own_2, send_2 = weight_partials(block, cots, spread, orders[1])
    other_2 = lax.ppermute(send_2, "rows", core_swap())

    early = [(own[48 * n : 48 * n + 48] + other[48 * n : 48 * n + 48]).astype(BF16) for n in range(2)]
    late = (own_2[:48] + other_2[:48]).astype(BF16)
    block, *early = lax.optimization_barrier((block, *early))
    received = [lax.ppermute(value, "rows", x_shift(k)) for value, k in zip(early, groups[0])]
    block, late = lax.optimization_barrier((block, late))
    received.append(lax.ppermute(late, "rows", x_shift(3)))
    input_grad = input_gradient(
        block,
        cotangent.reshape(2, 2 * columns, width),
        following.reshape(2, 2 * columns, width),
        cot_up,
        cot_dn,
        taps,
        flat,
        gamma,
    )
    input_grad, *received = lax.optimization_barrier((input_grad, *received))
    total = own_2[48:] + other_2[48:]
    for value in received:
        total = total + value.astype(F32)
    for bits in (1, 2, 6):
        half = total.shape[0] // 2
        pairs = rows_perm(lambda z, x, c: (z ^ bits, x, c))
        total = total[:half] + lax.ppermute(total[half:].astype(BF16), "rows", pairs).astype(F32)
    mine = total.reshape(6, 27, PART)
    count = pixels * lax.axis_size("tm") * lax.axis_size("rows")
    weight_grad = jnp.transpose(mine, (2, 1, 0)) * (1.0 / math.sqrt(count))
    return input_grad.reshape(features.shape), weight_grad


def solution(mesh):
    placed = (P("tm", "rows", None, None), P("tm", "rows", None, None), P(), P())
    return jax.shard_map(
        body,
        mesh=mesh,
        in_specs=placed,
        out_specs=(P("tm", "rows", None, None), P("tm", None, "rows")),
        check_vma=False,
    )
```

```python
import math

import jax
import jax.numpy as jnp
from jax import lax
from jax.experimental import pallas as pl
from jax.experimental.pallas import tpu as pltpu
from jax.sharding import PartitionSpec as P

F32, BF16 = jnp.float32, jnp.bfloat16
VMEM_LIMIT, VMEM_SMALL = 40 * 1024 * 1024, 26 * 1024 * 1024
C, COLS, PART, LANES = 384, 160, 96, 128
ZS, XS, YS = 8, 4, 4
NT = (((1,), (1,)), ((), ()))


def rows_perm(move):
    pairs = []
    for z in range(ZS):
        for x in range(XS):
            for c in range(2):
                z2, x2, c2 = move(z, x, c)
                pairs.append(((z * XS + x) * 2 + c, (z2 * XS + x2) * 2 + c2))
    return pairs


def x_shift(steps):
    return rows_perm(lambda z, x, c: (z, (x + steps) % XS, c))


def core_swap():
    return rows_perm(lambda z, x, c: (z, x, 1 - c))


def y_shift(steps):
    return [(i, (i + steps) % YS) for i in range(YS)]


def line(count, steps):
    return [(i, i + steps) for i in range(count) if 0 <= i + steps < count]


def activation_kernel(y_ref, features_ref, gamma_ref, *out_refs):
    floats = features_ref[...].astype(F32)
    inverse = lax.rsqrt(jnp.mean(floats * floats, axis=-1, keepdims=True) + 1e-6)
    pre_act = floats * inverse * gamma_ref[...][None, :]
    active = pre_act * jax.nn.sigmoid(pre_act)
    for part in range(YS):
        lanes = slice(part * PART, (part + 1) * PART)
        lines = [active[q * COLS : (q + 1) * COLS, lanes] for q in range(4)]
        piece = jnp.concatenate(lines, axis=1).astype(BF16)
        place = lax.rem(part - y_ref[0] + YS, YS)
        for k in range(YS):

            @pl.when(place == k)
            def _():
                out_refs[k][...] = piece


def activations(y, features, gamma):
    return pl.pallas_call(
        activation_kernel,
        in_specs=[pl.BlockSpec(memory_space=pltpu.SMEM)] + [pl.BlockSpec(memory_space=pltpu.VMEM)] * 2,
        out_shape=[jax.ShapeDtypeStruct((COLS, C), BF16)] * YS,
        compiler_params=pltpu.CompilerParams(vmem_limit_bytes=VMEM_LIMIT),
    )(y, features, gamma)


def halo_kernel(a0, a1, a2, a3, own, up, dn):
    acts = (a0, a1, a2, a3)
    for out, h in ((up, 1), (dn, 0)):
        for f in range(2):
            at = (f * 2 + h) * PART
            lines = [act[:, at : at + PART] for act in acts]
            out[f] = jnp.concatenate(lines, axis=1)
            out[2 + f] = own[f, h]


def halo_rows(acts, own):
    return pl.pallas_call(
        halo_kernel,
        in_specs=[pl.BlockSpec(memory_space=pltpu.VMEM)] * 5,
        out_specs=[pl.BlockSpec(memory_space=pltpu.VMEM)] * 2,
        out_shape=[jax.ShapeDtypeStruct((4, COLS, C), BF16)] * 2,
        compiler_params=pltpu.CompilerParams(vmem_limit_bytes=VMEM_SMALL),
    )(*acts, own)


def spread_kernel(a0, a1, a2, a3, up, dn, spread):
    acts = (a0, a1, a2, a3)
    column = lax.broadcasted_iota(jnp.int32, (4 * COLS, LANES), 0) % COLS
    blank = jnp.zeros((4 * COLS, LANES - PART), F32)
    for k in range(4):
        for f in range(2):
            lines = [
                up[f, :, k * PART : (k + 1) * PART],
                acts[k][:, f * 2 * PART : (f * 2 + 1) * PART],
                acts[k][:, (f * 2 + 1) * PART : (f * 2 + 2) * PART],
                dn[f, :, k * PART : (k + 1) * PART],
            ]
            floats = jnp.concatenate(lines, axis=0).astype(F32)
            floats = jnp.concatenate([floats, blank], axis=1)
            value = floats.astype(BF16)
            left = jnp.where(column == 0, 0.0, pltpu.roll(floats, 1, 0)).astype(BF16)
            right = jnp.where(column == COLS - 1, 0.0, pltpu.roll(floats, 4 * COLS - 1, 0)).astype(BF16)
            places = [(4 - k) * 2 + f] + ([f] if k == 0 else [])
            for place in places:
                rows = slice(place * 320, place * 320 + 320)
                for b in range(3):
                    for e, part in enumerate((left, value, right)):
                        at = (b * 3 + e) * LANES
                        spread[rows, at : at + LANES] = part[b * COLS : (b + 2) * COLS]


def spread_windows(acts, up, dn):
    return pl.pallas_call(
        spread_kernel,
        in_specs=[pl.BlockSpec(memory_space=pltpu.VMEM)] * 6,
        out_specs=pl.BlockSpec(memory_space=pltpu.VMEM),
        out_shape=jax.ShapeDtypeStruct((10 * 320, 9 * LANES), BF16),
        compiler_params=pltpu.CompilerParams(vmem_limit_bytes=VMEM_SMALL),
    )(*acts, up, dn)


def weight_kernel(y_ref, c3, c2a, c2b, c1, c0, spread, order_ref, own, send, cot):
    y = y_ref[0]
    order = order_ref[...]
    rows = order.shape[0]
    for k, pieces in enumerate(((c0,), (c1,), (c2a, c2b), (c3,))):
        first = lax.rem(y - k + 4, 4) == 0
        blocks = [
            lax.dot_general(order, piece[...], NT, preferred_element_type=F32).astype(BF16)
            for piece in pieces
        ]
        block = blocks[0] if len(blocks) == 1 else jnp.concatenate(blocks, axis=1)
        blank = jnp.zeros_like(block)
        frame = lax.broadcasted_iota(jnp.int32, block.shape, 1)
        at = (3 - k) * 640
        cot[2, :, at : at + 640] = block
        cot[1, :, at : at + 640] = jnp.where(first & (frame < 320), blank, block)
        cot[0, :, at : at + 640] = jnp.where(first, blank, block)
    pieces = []
    for a in range(3):
        value = jnp.dot(
            cot[a], spread[a * 320 : a * 320 + 2560, :], preferred_element_type=F32
        )
        pieces += [value[:, s * LANES : s * LANES + PART] for s in range(9)]
    packed = jnp.concatenate(pieces, axis=1)
    own[...] = packed[: rows // 2]
    send[...] = packed[rows // 2 :]


def weight_partials(y, cots, spread, order):
    rows = order.shape[0]
    shape = (rows // 2, 27 * PART)
    return pl.pallas_call(
        weight_kernel,
        in_specs=[pl.BlockSpec(memory_space=pltpu.SMEM)] + [pl.BlockSpec(memory_space=pltpu.VMEM)] * 7,
        out_specs=[pl.BlockSpec(memory_space=pltpu.VMEM)] * 2,
        out_shape=[jax.ShapeDtypeStruct(shape, F32)] * 2,
        scratch_shapes=[pltpu.VMEM((3, rows, 2560), BF16)],
        compiler_params=pltpu.CompilerParams(vmem_limit_bytes=VMEM_SMALL),
        cost_estimate=pl.CostEstimate(flops=28 * rows * 2560 * 256 * 2, bytes_accessed=8_000_000, transcendentals=0),
    )(y, *cots, spread, order)


def input_products(centre, edges, taps_ref, side, ext, lead, keep):
    step = pl.program_id(0)

    @pl.when(step == 0)
    def _():
        for f in range(2):
            for rows, value in (
                (slice(0, COLS), edges[0, f]),
                (slice(COLS, 3 * COLS), centre[f]),
                (slice(3 * COLS, 4 * COLS), edges[1, f]),
            ):
                ext[f, rows] = jnp.where(keep, value, jnp.zeros_like(value))

    weights = jnp.concatenate(
        [jnp.concatenate([taps_ref[0, b, e] for b in range(3)], axis=1) for e in range(3)], axis=0
    )

    def product(frames):
        rows = []
        for f in frames:
            pieces = [ext[f, (2 - b) * COLS : (4 - b) * COLS] for b in range(3)]
            rows.append(jnp.concatenate(pieces, axis=1))
        value = rows[0] if len(rows) == 1 else jnp.concatenate(rows, axis=0)
        return lax.dot_general(value, weights, NT, preferred_element_type=F32)

    @pl.when(step == 0)
    def _():
        if lead is None:
            side[...] = product((0, 1))
        else:
            side[...] = lead[...] + product((0, 1))

    @pl.when(step == 1)
    def _():
        if lead is None:
            side[: 2 * COLS] += product((1,))
        else:
            side[2 * COLS :] += product((0,))


def first_input_kernel(centre, edges, taps_ref, side, ext):
    input_products(centre, edges, taps_ref, side, ext, None, True)


def last_input_kernel(y_ref, centre, edges, taps_ref, lead, features_ref, gamma_ref, out_ref, ext, side):
    input_products(centre, edges, taps_ref, side, ext, lead, y_ref[0] != 3)

    @pl.when(pl.program_id(0) == 1)
    def _():
        column = lax.broadcasted_iota(jnp.int32, (4 * COLS, C), 0) % COLS
        grad_act = side[:, C : 2 * C]
        grad_act += jnp.where(column == COLS - 1, 0.0, pltpu.roll(side[:, :C], 4 * COLS - 1, 0))
        grad_act += jnp.where(column == 0, 0.0, pltpu.roll(side[:, 2 * C :], 1, 0))
        gamma = gamma_ref[...][None, :]
        floats = features_ref[...].astype(F32)
        inverse = lax.rsqrt(jnp.mean(floats * floats, axis=-1, keepdims=True) + 1e-6)
        normed = floats * inverse
        pre_act = normed * gamma
        sigma = jax.nn.sigmoid(pre_act)
        grad_norm = grad_act * sigma * (1.0 + pre_act * (1.0 - sigma)) * gamma
        inner = jnp.mean(grad_norm * normed, axis=-1, keepdims=True)
        out_ref[...] = (inverse * (grad_norm - normed * inner)).astype(BF16)


def whole(*shape):
    return pl.BlockSpec(shape, lambda step: (0,) * len(shape))


def first_input(own, edges, taps):
    return pl.pallas_call(
        first_input_kernel,
        grid=(2,),
        in_specs=[
            whole(2, 2 * COLS, C),
            whole(2, 2, COLS, C),
            pl.BlockSpec((1, 3, 3, C, C), lambda step: (2 - step, 0, 0, 0, 0)),
        ],
        out_specs=whole(4 * COLS, 3 * C),
        out_shape=jax.ShapeDtypeStruct((4 * COLS, 3 * C), F32),
        scratch_shapes=[pltpu.VMEM((2, 4 * COLS, C), BF16)],
        compiler_params=pltpu.CompilerParams(vmem_limit_bytes=VMEM_SMALL),
        cost_estimate=pl.CostEstimate(flops=27 * 640 * C * C, bytes_accessed=8_000_000, transcendentals=0),
    )(own, edges, taps)


def last_input(y, following, beyond, taps, lead, features, gamma):
    return pl.pallas_call(
        last_input_kernel,
        grid=(2,),
        in_specs=[
            pl.BlockSpec(memory_space=pltpu.SMEM),
            whole(2, 2 * COLS, C),
            whole(2, 2, COLS, C),
            pl.BlockSpec((1, 3, 3, C, C), lambda step: (step, 0, 0, 0, 0)),
            whole(4 * COLS, 3 * C),
            whole(4 * COLS, C),
            whole(C),
        ],
        out_specs=whole(4 * COLS, C),
        out_shape=jax.ShapeDtypeStruct((4 * COLS, C), BF16),
        scratch_shapes=[
            pltpu.VMEM((2, 4 * COLS, C), BF16),
            pltpu.VMEM((4 * COLS, 3 * C), F32),
        ],
        compiler_params=pltpu.CompilerParams(vmem_limit_bytes=VMEM_SMALL),
        cost_estimate=pl.CostEstimate(flops=27 * 640 * C * C, bytes_accessed=8_000_000, transcendentals=0),
    )(y, following, beyond, taps, lead, features, gamma)


def output_order(z, x, core, parts):
    row = jnp.arange(len(parts) * 96)
    c2, at, z2, j = row // (48 * len(parts)), row // 48 % len(parts), row // 6 % ZS, row % 6
    x2 = jnp.where(at == 0, parts[0], parts[1])
    bits = z2 // 4 ^ z2 // 2 % 2 * 2 ^ z2 % 2 * 6
    channel = (z ^ bits) * 48 + (x + x2) % XS * 12 + (core + c2) % 2 * 6 + j
    return (channel[:, None] == jnp.arange(C)[None, :]).astype(BF16)


def body(features, cotangent, gamma, kernel):
    frames, height, columns, width = features.shape
    pixels = frames * height * columns
    y, r = lax.axis_index("tm"), lax.axis_index("rows")
    z, x, core = r // (2 * XS), (r // 2) % XS, r % 2
    block = y.reshape(1).astype(jnp.int32)
    groups = ((2, 1), (3, 0))
    orders = [output_order(z, x, core, parts) for parts in groups]
    flat = features.reshape(pixels, width)
    taps = jnp.transpose(kernel, (1, 0, 2)).reshape(3, 3, 3, width, width)

    active = activations(block, flat, gamma)
    acts = [active[0]] + [lax.ppermute(active[k], "tm", y_shift(k)) for k in (1, 2, 3)]
    local, *acts = lax.optimization_barrier((cotangent, *acts))
    following = lax.ppermute(local, "tm", y_shift(3))
    previous = lax.ppermute(local, "tm", y_shift(1))
    rows_up, rows_dn = halo_rows(acts, local)
    rows_up = lax.ppermute(rows_up, "rows", line(64, 1))
    rows_dn = lax.ppermute(rows_dn, "rows", line(64, -1))
    edges = jnp.stack([rows_up[2:], rows_dn[2:]])
    far = [
        lax.ppermute(previous[0], "tm", y_shift(1)).reshape(pixels // 2, width),
        lax.ppermute(following[1], "tm", y_shift(3)).reshape(pixels // 2, width),
    ]
    spread = spread_windows(acts, rows_up, rows_dn)
    cots = [following.reshape(pixels, width), *far, previous.reshape(pixels, width), cotangent.reshape(pixels, width)]

    own, send = weight_partials(block, cots, spread, orders[0])
    other = lax.ppermute(send, "rows", core_swap())
    orders[1], own = lax.optimization_barrier((orders[1], own))
    own_2, send_2 = weight_partials(block, cots, spread, orders[1])
    other_2 = lax.ppermute(send_2, "rows", core_swap())

    early = [(own[48 * n : 48 * n + 48] + other[48 * n : 48 * n + 48]).astype(BF16) for n in range(2)]
    late = (own_2[:48] + other_2[:48]).astype(BF16)
    edges, own_rows, *early = lax.optimization_barrier((edges, cotangent, *early))
    received = [lax.ppermute(value, "rows", x_shift(k)) for value, k in zip(early, groups[0])]
    own_rows, late = lax.optimization_barrier((own_rows, late))
    received.append(lax.ppermute(late, "rows", x_shift(3)))
    beyond = lax.ppermute(edges, "tm", y_shift(3))
    lead = first_input(own_rows.reshape(2, 2 * columns, width), edges, taps)
    lead, *received = lax.optimization_barrier((lead, *received))
    total = own_2[48:] + other_2[48:]
    for value in received:
        total = total + value.astype(F32)
    for bits in (1, 2, 6):
        half = total.shape[0] // 2
        pairs = rows_perm(lambda z, x, c: (z ^ bits, x, c))
        sent = total[half:].astype(BF16)
        if bits == 1:
            sent, block = lax.optimization_barrier((sent, block))
        partner = lax.ppermute(sent, "rows", pairs)
        if bits == 1:
            input_grad = last_input(
                block, following.reshape(2, 2 * columns, width), beyond, taps, lead, flat, gamma
            )
            input_grad, partner = lax.optimization_barrier((input_grad, partner))
        total = total[:half] + partner.astype(F32)
    mine = total.reshape(6, 27, PART)
    count = pixels * lax.axis_size("tm") * lax.axis_size("rows")
    weight_grad = jnp.transpose(mine, (2, 1, 0)) * (1.0 / math.sqrt(count))
    return input_grad.reshape(features.shape), weight_grad


def solution(mesh):
    placed = (P("tm", "rows", None, None), P("tm", "rows", None, None), P(), P())
    return jax.shard_map(
        body,
        mesh=mesh,
        in_specs=placed,
        out_specs=(P("tm", "rows", None, None), P("tm", None, "rows")),
        check_vma=False,
    )
```

```python
import math

import jax
import jax.numpy as jnp
from jax import lax
from jax.experimental import pallas as pl
from jax.experimental.pallas import tpu as pltpu
from jax.sharding import PartitionSpec as P

F32, BF16 = jnp.float32, jnp.bfloat16
VMEM_LIMIT, VMEM_SMALL = 40 * 1024 * 1024, 26 * 1024 * 1024
C, COLS, PART, LANES = 384, 160, 96, 128
ZS, XS, YS = 8, 4, 4
NT = (((1,), (1,)), ((), ()))


def rows_perm(move):
    pairs = []
    for z in range(ZS):
        for x in range(XS):
            for c in range(2):
                z2, x2, c2 = move(z, x, c)
                pairs.append(((z * XS + x) * 2 + c, (z2 * XS + x2) * 2 + c2))
    return pairs


def x_shift(steps):
    return rows_perm(lambda z, x, c: (z, (x + steps) % XS, c))


def core_swap():
    return rows_perm(lambda z, x, c: (z, x, 1 - c))


def y_shift(steps):
    return [(i, (i + steps) % YS) for i in range(YS)]


def line(count, steps):
    return [(i, i + steps) for i in range(count) if 0 <= i + steps < count]


def activation_kernel(y_ref, features_ref, gamma_ref, *out_refs):
    floats = features_ref[...].astype(F32)
    inverse = lax.rsqrt(jnp.mean(floats * floats, axis=-1, keepdims=True) + 1e-6)
    pre_act = floats * inverse * gamma_ref[...][None, :]
    active = pre_act * jax.nn.sigmoid(pre_act)
    for part in range(YS):
        lanes = slice(part * PART, (part + 1) * PART)
        lines = [active[q * COLS : (q + 1) * COLS, lanes] for q in range(4)]
        piece = jnp.concatenate(lines, axis=1).astype(BF16)
        place = lax.rem(part - y_ref[0] + YS, YS)
        for k in range(YS):

            @pl.when(place == k)
            def _():
                out_refs[k][...] = piece


def activations(y, features, gamma):
    return pl.pallas_call(
        activation_kernel,
        in_specs=[pl.BlockSpec(memory_space=pltpu.SMEM)] + [pl.BlockSpec(memory_space=pltpu.VMEM)] * 2,
        out_shape=[jax.ShapeDtypeStruct((COLS, C), BF16)] * YS,
        compiler_params=pltpu.CompilerParams(vmem_limit_bytes=VMEM_LIMIT),
    )(y, features, gamma)


def halo_kernel(a0, a1, a2, a3, own, up, dn):
    acts = (a0, a1, a2, a3)
    for out, h in ((up, 1), (dn, 0)):
        for f in range(2):
            at = (f * 2 + h) * PART
            lines = [act[:, at : at + PART] for act in acts]
            out[f] = jnp.concatenate(lines, axis=1)
            out[2 + f] = own[f, h]


def halo_rows(acts, own):
    return pl.pallas_call(
        halo_kernel,
        in_specs=[pl.BlockSpec(memory_space=pltpu.VMEM)] * 5,
        out_specs=[pl.BlockSpec(memory_space=pltpu.VMEM)] * 2,
        out_shape=[jax.ShapeDtypeStruct((4, COLS, C), BF16)] * 2,
        compiler_params=pltpu.CompilerParams(vmem_limit_bytes=VMEM_SMALL),
    )(*acts, own)


def spread_kernel(a0, a1, a2, a3, up, dn, spread):
    acts = (a0, a1, a2, a3)
    column = lax.broadcasted_iota(jnp.int32, (4 * COLS, LANES), 0) % COLS
    blank = jnp.zeros((4 * COLS, LANES - PART), F32)
    for k in range(4):
        for f in range(2):
            lines = [
                up[f, :, k * PART : (k + 1) * PART],
                acts[k][:, f * 2 * PART : (f * 2 + 1) * PART],
                acts[k][:, (f * 2 + 1) * PART : (f * 2 + 2) * PART],
                dn[f, :, k * PART : (k + 1) * PART],
            ]
            floats = jnp.concatenate(lines, axis=0).astype(F32)
            floats = jnp.concatenate([floats, blank], axis=1)
            value = floats.astype(BF16)
            left = jnp.where(column == 0, 0.0, pltpu.roll(floats, 1, 0)).astype(BF16)
            right = jnp.where(column == COLS - 1, 0.0, pltpu.roll(floats, 4 * COLS - 1, 0)).astype(BF16)
            places = [(4 - k) * 2 + f] + ([f] if k == 0 else [])
            for place in places:
                rows = slice(place * 320, place * 320 + 320)
                for b in range(3):
                    for e, part in enumerate((left, value, right)):
                        at = (b * 3 + e) * LANES
                        spread[rows, at : at + LANES] = part[b * COLS : (b + 2) * COLS]


def spread_windows(acts, up, dn):
    return pl.pallas_call(
        spread_kernel,
        in_specs=[pl.BlockSpec(memory_space=pltpu.VMEM)] * 6,
        out_specs=pl.BlockSpec(memory_space=pltpu.VMEM),
        out_shape=jax.ShapeDtypeStruct((10 * 320, 9 * LANES), BF16),
        compiler_params=pltpu.CompilerParams(vmem_limit_bytes=VMEM_SMALL),
    )(*acts, up, dn)


def weight_kernel(y_ref, c3, c2a, c2b, c1, c0, spread, order_ref, own, send, cot):
    y = y_ref[0]
    order = order_ref[...]
    rows = order.shape[0]
    for k, pieces in enumerate(((c0,), (c1,), (c2a, c2b), (c3,))):
        first = lax.rem(y - k + 4, 4) == 0
        blocks = [
            lax.dot_general(order, piece[...], NT, preferred_element_type=F32).astype(BF16)
            for piece in pieces
        ]
        block = blocks[0] if len(blocks) == 1 else jnp.concatenate(blocks, axis=1)
        blank = jnp.zeros_like(block)
        frame = lax.broadcasted_iota(jnp.int32, block.shape, 1)
        at = (3 - k) * 640
        cot[2, :, at : at + 640] = block
        cot[1, :, at : at + 640] = jnp.where(first & (frame < 320), blank, block)
        cot[0, :, at : at + 640] = jnp.where(first, blank, block)
    pieces = []
    for a in range(3):
        value = jnp.dot(
            cot[a], spread[a * 320 : a * 320 + 2560, :], preferred_element_type=F32
        )
        pieces += [value[:, s * LANES : s * LANES + PART] for s in range(9)]
    packed = jnp.concatenate(pieces, axis=1)
    own[...] = packed[: rows // 2]
    send[...] = packed[rows // 2 :]


def weight_partials(y, cots, spread, order):
    rows = order.shape[0]
    shape = (rows // 2, 27 * PART)
    return pl.pallas_call(
        weight_kernel,
        in_specs=[pl.BlockSpec(memory_space=pltpu.SMEM)] + [pl.BlockSpec(memory_space=pltpu.VMEM)] * 7,
        out_specs=[pl.BlockSpec(memory_space=pltpu.VMEM)] * 2,
        out_shape=[jax.ShapeDtypeStruct(shape, F32)] * 2,
        scratch_shapes=[pltpu.VMEM((3, rows, 2560), BF16)],
        compiler_params=pltpu.CompilerParams(vmem_limit_bytes=VMEM_SMALL),
        cost_estimate=pl.CostEstimate(flops=28 * rows * 2560 * 256 * 2, bytes_accessed=8_000_000, transcendentals=0),
    )(y, *cots, spread, order)


def input_products(centre, edges, taps_ref, side, ext, lead, keep):
    step = pl.program_id(0)

    @pl.when(step == 0)
    def _():
        for f in range(2):
            for rows, value in (
                (slice(0, COLS), edges[0, f] if lead is None else jnp.zeros_like(centre[f, :COLS])),
                (slice(COLS, 3 * COLS), centre[f]),
                (slice(3 * COLS, 4 * COLS), edges[1, f] if lead is None else jnp.zeros_like(centre[f, :COLS])),
            ):
                ext[f, rows] = jnp.where(keep, value, jnp.zeros_like(value))

    weights = jnp.concatenate(
        [jnp.concatenate([taps_ref[0, b, e] for b in range(3)], axis=1) for e in range(3)], axis=0
    )

    def product(frames):
        rows = []
        for f in frames:
            pieces = [ext[f, (2 - b) * COLS : (4 - b) * COLS] for b in range(3)]
            rows.append(jnp.concatenate(pieces, axis=1))
        value = rows[0] if len(rows) == 1 else jnp.concatenate(rows, axis=0)
        return lax.dot_general(value, weights, NT, preferred_element_type=F32)

    @pl.when(step == 0)
    def _():
        if lead is None:
            side[...] = product((0, 1))
        else:
            side[...] = lead[...] + product((0, 1))

    @pl.when(step == 1)
    def _():
        if lead is None:
            side[: 2 * COLS] += product((1,))
        else:
            side[2 * COLS :] += product((0,))


def first_input_kernel(centre, edges, taps_ref, side, ext):
    input_products(centre, edges, taps_ref, side, ext, None, True)


def middle_input_kernel(y_ref, centre, taps_ref, lead, side, ext):
    input_products(centre, None, taps_ref, side, ext, lead, y_ref[0] != 3)


def middle_input(y, following, taps, lead):
    return pl.pallas_call(
        middle_input_kernel,
        grid=(2,),
        in_specs=[
            pl.BlockSpec(memory_space=pltpu.SMEM),
            whole(2, 2 * COLS, C),
            pl.BlockSpec((1, 3, 3, C, C), lambda step: (step, 0, 0, 0, 0)),
            whole(4 * COLS, 3 * C),
        ],
        out_specs=whole(4 * COLS, 3 * C),
        out_shape=jax.ShapeDtypeStruct((4 * COLS, 3 * C), F32),
        scratch_shapes=[pltpu.VMEM((2, 4 * COLS, C), BF16)],
        compiler_params=pltpu.CompilerParams(vmem_limit_bytes=VMEM_SMALL),
        cost_estimate=pl.CostEstimate(flops=27 * 640 * C * C, bytes_accessed=8_000_000, transcendentals=0),
    )(y, following, taps, lead)


def last_input_kernel(y_ref, edges, taps_ref, lead, features_ref, gamma_ref, out_ref, side):
    keep = y_ref[0] != 3

    def add(f, frame):
        for h, b in ((0, 2), (1, 0)):
            value = edges[h, frame]
            value = jnp.where(keep, value, jnp.zeros_like(value))
            weights = jnp.concatenate([taps_ref[0, b, e] for e in range(3)], axis=0)
            rows = slice((f * 2 + h) * COLS, (f * 2 + h + 1) * COLS)
            side[rows] += lax.dot_general(value, weights, NT, preferred_element_type=F32)

    @pl.when(pl.program_id(0) == 0)
    def _():
        side[...] = lead[...]
        add(0, 0)
        add(1, 1)

    @pl.when(pl.program_id(0) == 1)
    def _():
        add(1, 0)

    @pl.when(pl.program_id(0) == 1)
    def _():
        column = lax.broadcasted_iota(jnp.int32, (4 * COLS, C), 0) % COLS
        grad_act = side[:, C : 2 * C]
        grad_act += jnp.where(column == COLS - 1, 0.0, pltpu.roll(side[:, :C], 4 * COLS - 1, 0))
        grad_act += jnp.where(column == 0, 0.0, pltpu.roll(side[:, 2 * C :], 1, 0))
        gamma = gamma_ref[...][None, :]
        floats = features_ref[...].astype(F32)
        inverse = lax.rsqrt(jnp.mean(floats * floats, axis=-1, keepdims=True) + 1e-6)
        normed = floats * inverse
        pre_act = normed * gamma
        sigma = jax.nn.sigmoid(pre_act)
        grad_norm = grad_act * sigma * (1.0 + pre_act * (1.0 - sigma)) * gamma
        inner = jnp.mean(grad_norm * normed, axis=-1, keepdims=True)
        out_ref[...] = (inverse * (grad_norm - normed * inner)).astype(BF16)


def whole(*shape):
    return pl.BlockSpec(shape, lambda step: (0,) * len(shape))


def first_input(own, edges, taps):
    return pl.pallas_call(
        first_input_kernel,
        grid=(2,),
        in_specs=[
            whole(2, 2 * COLS, C),
            whole(2, 2, COLS, C),
            pl.BlockSpec((1, 3, 3, C, C), lambda step: (2 - step, 0, 0, 0, 0)),
        ],
        out_specs=whole(4 * COLS, 3 * C),
        out_shape=jax.ShapeDtypeStruct((4 * COLS, 3 * C), F32),
        scratch_shapes=[pltpu.VMEM((2, 4 * COLS, C), BF16)],
        compiler_params=pltpu.CompilerParams(vmem_limit_bytes=VMEM_SMALL),
        cost_estimate=pl.CostEstimate(flops=27 * 640 * C * C, bytes_accessed=8_000_000, transcendentals=0),
    )(own, edges, taps)


def last_input(y, beyond, taps, lead, features, gamma):
    return pl.pallas_call(
        last_input_kernel,
        grid=(2,),
        in_specs=[
            pl.BlockSpec(memory_space=pltpu.SMEM),
            whole(2, 2, COLS, C),
            pl.BlockSpec((1, 3, 3, C, C), lambda step: (step, 0, 0, 0, 0)),
            whole(4 * COLS, 3 * C),
            whole(4 * COLS, C),
            whole(C),
        ],
        out_specs=whole(4 * COLS, C),
        out_shape=jax.ShapeDtypeStruct((4 * COLS, C), BF16),
        scratch_shapes=[
            pltpu.VMEM((4 * COLS, 3 * C), F32),
        ],
        compiler_params=pltpu.CompilerParams(vmem_limit_bytes=VMEM_SMALL),
        cost_estimate=pl.CostEstimate(flops=27 * 640 * C * C, bytes_accessed=8_000_000, transcendentals=0),
    )(y, beyond, taps, lead, features, gamma)


def output_order(z, x, core, parts):
    row = jnp.arange(len(parts) * 96)
    c2, at, z2, j = row // (48 * len(parts)), row // 48 % len(parts), row // 6 % ZS, row % 6
    x2 = jnp.where(at == 0, parts[0], parts[1])
    bits = z2 // 4 ^ z2 // 2 % 2 * 2 ^ z2 % 2 * 6
    channel = (z ^ bits) * 48 + (x + x2) % XS * 12 + (core + c2) % 2 * 6 + j
    return (channel[:, None] == jnp.arange(C)[None, :]).astype(BF16)


def body(features, cotangent, gamma, kernel):
    frames, height, columns, width = features.shape
    pixels = frames * height * columns
    y, r = lax.axis_index("tm"), lax.axis_index("rows")
    z, x, core = r // (2 * XS), (r // 2) % XS, r % 2
    block = y.reshape(1).astype(jnp.int32)
    groups = ((2, 1), (3, 0))
    orders = [output_order(z, x, core, parts) for parts in groups]
    flat = features.reshape(pixels, width)
    taps = jnp.transpose(kernel, (1, 0, 2)).reshape(3, 3, 3, width, width)

    active = activations(block, flat, gamma)
    acts = [active[0]] + [lax.ppermute(active[k], "tm", y_shift(k)) for k in (1, 2, 3)]
    local, *acts = lax.optimization_barrier((cotangent, *acts))
    following = lax.ppermute(local, "tm", y_shift(3))
    previous = lax.ppermute(local, "tm", y_shift(1))
    rows_up, rows_dn = halo_rows(acts, local)
    rows_up = lax.ppermute(rows_up, "rows", line(64, 1))
    rows_dn = lax.ppermute(rows_dn, "rows", line(64, -1))
    edges = jnp.stack([rows_up[2:], rows_dn[2:]])
    far = [
        lax.ppermute(previous[0], "tm", y_shift(1)).reshape(pixels // 2, width),
        lax.ppermute(following[1], "tm", y_shift(3)).reshape(pixels // 2, width),
    ]
    spread = spread_windows(acts, rows_up, rows_dn)
    cots = [following.reshape(pixels, width), *far, previous.reshape(pixels, width), cotangent.reshape(pixels, width)]

    own, send = weight_partials(block, cots, spread, orders[0])
    other = lax.ppermute(send, "rows", core_swap())
    orders[1], own = lax.optimization_barrier((orders[1], own))
    own_2, send_2 = weight_partials(block, cots, spread, orders[1])
    other_2 = lax.ppermute(send_2, "rows", core_swap())

    early = [(own[48 * n : 48 * n + 48] + other[48 * n : 48 * n + 48]).astype(BF16) for n in range(2)]
    late = (own_2[:48] + other_2[:48]).astype(BF16)
    edges, own_rows, *early = lax.optimization_barrier((edges, cotangent, *early))
    received = [lax.ppermute(value, "rows", x_shift(k)) for value, k in zip(early, groups[0])]
    own_rows, late = lax.optimization_barrier((own_rows, late))
    received.append(lax.ppermute(late, "rows", x_shift(3)))
    beyond = lax.ppermute(edges, "tm", y_shift(3))
    lead = first_input(own_rows.reshape(2, 2 * columns, width), edges, taps)
    lead = middle_input(block, following.reshape(2, 2 * columns, width), taps, lead)
    lead, *received = lax.optimization_barrier((lead, *received))
    total = own_2[48:] + other_2[48:]
    for value in received:
        total = total + value.astype(F32)
    for bits in (1, 2, 6):
        half = total.shape[0] // 2
        pairs = rows_perm(lambda z, x, c: (z ^ bits, x, c))
        sent = total[half:].astype(BF16)
        if bits == 1:
            sent, block = lax.optimization_barrier((sent, block))
        partner = lax.ppermute(sent, "rows", pairs)
        if bits == 1:
            input_grad = last_input(
                block, beyond, taps, lead, flat, gamma
            )
            input_grad, partner = lax.optimization_barrier((input_grad, partner))
        total = total[:half] + partner.astype(F32)
    mine = total.reshape(6, 27, PART)
    count = pixels * lax.axis_size("tm") * lax.axis_size("rows")
    weight_grad = jnp.transpose(mine, (2, 1, 0)) * (1.0 / math.sqrt(count))
    return input_grad.reshape(features.shape), weight_grad


def solution(mesh):
    placed = (P("tm", "rows", None, None), P("tm", "rows", None, None), P(), P())
    return jax.shard_map(
        body,
        mesh=mesh,
        in_specs=placed,
        out_specs=(P("tm", "rows", None, None), P("tm", None, "rows")),
        check_vma=False,
    )
```
